128 devices in a mesh: fsdp: 128 (over y, x, z, core).
Axes of the slice: x: 4, y: 4, z: 4, core: 2. Of those that a mesh axis runs over, the one named last changes fastest.
Arguments:
- momentum: float32 [64, 1024, 3584], P(None, 'fsdp'), may hold values from -40 to 40
- gradient: bfloat16 [64, 1024, 3584], P(None, 'fsdp'), may hold values from -40 to 40
Outputs:
- new_momentum: float32 [64, 1024, 3584], P(None, 'fsdp')
- update: bfloat16 [64, 1024, 3584], P(None, 'fsdp')
The draws below stay inside these ranges and needn't reach their ends.
All inputs are finite; a program needn't handle non-finite values.
Results may differ from the reference program's by a relative error of at most 0.02.
Values may be sent and summed in bfloat16 or wider, within the bound.
No kernel may reach another device: no remote copies, remote signals or barrier semaphores. Data moves between devices by JAX's collectives and lax.ppermute only.
A program may use at most 128 MiB of HBM per device.

```python
import jax
import jax.numpy as jnp
from jax import lax

D = 3584
FF = 1024
ITERS = 3
MATRICES = 64


def half_weight(key):
    chosen = jax.random.randint(key, (MATRICES, 1, 1), 0, 2)
    columns = jnp.arange(D, dtype=jnp.int32).reshape(1, 1, D)
    upper = (columns >= D // 2).astype(jnp.int32)
    return jnp.where(upper == chosen, 3.0, 1.0).astype(jnp.float32)


def scaled_field(key, weight):
    first, second, third = jax.random.split(key, 3)
    base = jnp.clip(jax.random.normal(first, (MATRICES, FF, D), jnp.float32), -4.0, 4.0)
    row_scale = jnp.exp(jax.random.uniform(second, (MATRICES, FF, 1), jnp.float32) * jnp.log(10.0))
    col_scale = jnp.exp(jax.random.uniform(third, (MATRICES, 1, D), jnp.float32) * jnp.log(10.0))
    return base * row_scale * col_scale * weight / 30.0


def draw_momentum(key, part):
    weight = half_weight(key)
    key = jax.random.fold_in(key, 1)
    return scaled_field(key, weight).astype(jnp.float32)


def draw_gradient(key, part):
    weight = half_weight(key)
    key = jax.random.fold_in(key, 2)
    return scaled_field(key, weight).astype(jnp.bfloat16)


def setup_inputs(seed: int = 0) -> dict:
    seeds = jax.random.split(jax.random.key(seed), 3)
    return {
        "momentum": draw_momentum(jax.random.fold_in(seeds[2], 71), 0),
        "gradient": draw_gradient(jax.random.fold_in(seeds[2], 71), 0),
    }


def orthogonalize(steer):
    values = steer.astype(jnp.float32)
    inverse = 1.0 / (jnp.sqrt(jnp.sum(values * values)) + 1e-07)
    x = (values * inverse).astype(jnp.bfloat16)
    for step in range(ITERS):
        gram = lax.dot_general(x, x, (((1,), (1,)), ((), ())), preferred_element_type=jnp.float32).astype(jnp.bfloat16)
        square = jnp.dot(gram, gram, preferred_element_type=jnp.float32)
        mix = (-4.775 * gram.astype(jnp.float32) + 2.0315 * square).astype(jnp.bfloat16)
        x = (3.4445 * x.astype(jnp.float32) + jnp.dot(mix, x, preferred_element_type=jnp.float32)).astype(jnp.bfloat16)
    factor = 0.2 * max(FF, D) ** 0.5
    return (x.astype(jnp.float32) * factor).astype(jnp.bfloat16)

def reference(momentum, gradient):
    new_momentum = 0.95 * momentum + gradient.astype(jnp.float32)
    steer = (gradient.astype(jnp.float32) + 0.95 * new_momentum).astype(jnp.bfloat16)
    update = lax.map(orthogonalize, steer)
    return (new_momentum, update)
```

```python
import jax
import jax.numpy as jnp
from jax import lax
from jax.experimental import pallas as pl
from jax.experimental.pallas import tpu as pltpu
from jax.sharding import PartitionSpec as P

D = 3584
FF = 1024
ITERS = 3
LINEAR, CUBIC, QUINTIC = 3.4445, -4.775, 2.0315
FACTOR = 0.2 * max(FF, D) ** 0.5
TILE = 256
SIDE = FF // TILE
PAIRS = [(i, j) for j in range(SIDE) for i in range(j + 1)]
MIB = 2**20


def cost(flops, moved):
    return pl.CostEstimate(flops=flops, bytes_accessed=moved, transcendentals=0)


def span(i, size=TILE):
    return slice(i * size, (i + 1) * size)


def partner(x, axis, apart):
    return lax.ppermute(x, axis, [(i, i ^ 1 << apart) for i in range(lax.axis_size(axis))])


STEER_PARTS = 8


def steer_kernel(momentum, gradient, steer, m_buf, g_buf, s_buf, m_sem, g_sem, s_sem):
    mats, rows, width = m_buf.shape
    half = width // 2
    group = mats // STEER_PARTS
    arriving = []
    for c in range(STEER_PARTS):
        at = pl.ds(c * group, group)
        pair = (
            pltpu.make_async_copy(momentum.at[at], m_buf.at[at], m_sem.at[c]),
            pltpu.make_async_copy(gradient.at[at], g_buf.at[at], g_sem.at[c]),
        )
        for copy in pair:
            copy.start()
        arriving.append(pair)
    leaving = []
    for c in range(STEER_PARTS):
        for copy in arriving[c]:
            copy.wait()

        @pl.loop(c * group, (c + 1) * group)
        def _(m):
            g = g_buf[m].astype(jnp.float32)
            moved = 0.95 * m_buf[m] + g
            value = (g + 0.95 * moved).astype(jnp.bfloat16)
            s_buf[m, 0] = value[:, :half]
            s_buf[m, 1] = value[:, half:]

        at = pl.ds(c * group, group)
        copy = pltpu.make_async_copy(s_buf.at[at], steer.at[at], s_sem.at[c])
        copy.start()
        leaving.append(copy)
    for copy in leaving:
        copy.wait()


def steer_pieces(momentum, gradient):
    mats, rows, width = momentum.shape
    shape = (mats, 2, rows, width // 2)
    anywhere = pl.BlockSpec(memory_space=pl.ANY)
    dma = pltpu.SemaphoreType.DMA((STEER_PARTS,))
    return pl.pallas_call(
        steer_kernel,
        out_shape=jax.ShapeDtypeStruct(shape, jnp.bfloat16),
        in_specs=[anywhere] * 2,
        out_specs=anywhere,
        scratch_shapes=[
            pltpu.VMEM(momentum.shape, jnp.float32),
            pltpu.VMEM(gradient.shape, jnp.bfloat16),
            pltpu.VMEM(shape, jnp.bfloat16),
            dma,
            dma,
            dma,
        ],
        compiler_params=pltpu.CompilerParams(vmem_limit_bytes=56 * MIB),
        cost_estimate=cost(4 * momentum.size, 8 * momentum.size),
        name="steer",
    )(momentum, gradient).reshape(mats * 2, rows, width // 2)


def gram_kernel(x, own, sent, x_buf, sem):
    arriving = []
    for i in range(SIDE):
        copy = pltpu.make_async_copy(x.at[span(i)], x_buf.at[span(i)], sem.at[i])
        copy.start()
        arriving.append(copy)
    for j in range(SIDE):
        arriving[j].wait()
        value = lax.dot_general(
            x_buf[0 : (j + 1) * TILE],
            x_buf[span(j)],
            (((1,), (1,)), ((), ())),
            preferred_element_type=jnp.float32,
        )
        at = slice(j * (j + 1) // 2 * TILE, (j + 1) * (j + 2) // 2 * TILE)
        own[at] = value
        sent[at] = value.astype(jnp.bfloat16)


def gram_half(x):
    rows, part = x.shape
    shape = (len(PAIRS) * TILE, TILE)
    return pl.pallas_call(
        gram_kernel,
        out_shape=(
            jax.ShapeDtypeStruct(shape, jnp.float32),
            jax.ShapeDtypeStruct(shape, jnp.bfloat16),
        ),
        in_specs=[pl.BlockSpec(memory_space=pl.ANY)],
        scratch_shapes=[
            pltpu.VMEM((rows, part), jnp.bfloat16),
            pltpu.SemaphoreType.DMA((SIDE,)),
        ],
        compiler_params=pltpu.CompilerParams(vmem_limit_bytes=32 * MIB),
        cost_estimate=cost(2 * len(PAIRS) * TILE * TILE * part, rows * part * 2 + len(PAIRS) * TILE * TILE * 6),
        name="gram",
    )(x)


def update_kernel(x, own, other, out, x_buf, g, h, s, w, m0, m1, x_sem):
    n, part = x_buf.shape
    loading = pltpu.make_async_copy(x, x_buf, x_sem)
    loading.start()
    here = lax.broadcasted_iota(jnp.int32, (TILE, TILE), 0) == lax.broadcasted_iota(
        jnp.int32, (TILE, TILE), 1
    )
    total = jnp.zeros((1, 1), jnp.float32)
    for k, (i, j) in enumerate(PAIRS):
        block = own[span(k)] + other[span(k)].astype(jnp.float32)
        narrow = block.astype(jnp.bfloat16)
        g[span(i), span(j)] = narrow
        if i == j:
            block = jnp.where(here, block, 0.0)
            block = jnp.sum(block, axis=0, keepdims=True)
            total = total + jnp.sum(block, axis=1, keepdims=True)
        else:
            g[span(j), span(i)] = narrow.T
    inverse = 1.0 / (jnp.sqrt(total) + 1e-07)
    factor = inverse * FACTOR
    square = inverse * inverse

    def product(left, right, store, rest):
        for j in range(SIDE):
            at = (slice(0, (j + 1) * TILE), span(j))
            value = jnp.dot(left[at[0], :], right[:, at[1]], preferred_element_type=jnp.float32)
            narrow = rest(value, at).astype(jnp.bfloat16)
            store[at] = narrow
            for i in range(j):
                store[span(j), span(i)] = narrow[span(i)].T

    def wide(ref, at):
        return ref[at].astype(jnp.float32)


    product(g, g, m0, lambda v, at: square * (CUBIC * wide(g, at) + square * (QUINTIC * v)))
    product(m0, g, w, lambda v, at: square * (LINEAR * wide(g, at) + v))
    product(m0, w, h, lambda v, at: LINEAR * wide(w, at) + v)
    product(h, h, m1, lambda v, at: CUBIC * wide(h, at) + QUINTIC * v)
    product(m1, h, w, lambda v, at: LINEAR * wide(h, at) + v)
    product(m1, w, g, lambda v, at: LINEAR * wide(w, at) + v)
    product(m1, m0, s, lambda v, at: LINEAR * (wide(m0, at) + wide(m1, at)) + v)
    product(g, g, m0, lambda v, at: CUBIC * wide(g, at) + QUINTIC * v)
    product(m0, s, h, lambda v, at: LINEAR * wide(s, at) + LINEAR * LINEAR * wide(m0, at) + v)
    loading.wait()
    for i in range(SIDE):
        value = jnp.dot(h[span(i), :], x_buf[...], preferred_element_type=jnp.float32)
        value = value + LINEAR**3 * x_buf[span(i)].astype(jnp.float32)
        out[span(i)] = (value * factor).astype(jnp.bfloat16)


def update_half(x, own, other):
    n, part = x.shape
    anywhere = pl.BlockSpec(memory_space=pl.ANY)
    square = pltpu.VMEM((n, n), jnp.bfloat16)
    return pl.pallas_call(
        update_kernel,
        out_shape=jax.ShapeDtypeStruct((n, part), jnp.bfloat16),
        in_specs=[
            anywhere,
            pl.BlockSpec(memory_space=pltpu.VMEM),
            pl.BlockSpec(memory_space=pltpu.VMEM),
        ],
        out_specs=pl.BlockSpec(memory_space=pltpu.VMEM),
        scratch_shapes=[
            pltpu.VMEM((n, part), jnp.bfloat16),
            *[square] * 6,
            pltpu.SemaphoreType.DMA,
        ],
        compiler_params=pltpu.CompilerParams(vmem_limit_bytes=40 * MIB),
        cost_estimate=cost(2 * n * n * (9 * n + part), n * part * 4 + n * n * 6),
        name="update",
    )(x, own, other)


def exchange(x):
    return lax.all_to_all(x, "fsdp", split_axis=0, concat_axis=0, tiled=True)


def local(momentum, gradient):
    count = lax.axis_size("fsdp")
    mats, rows, width = momentum.shape
    half = width // 2
    x = exchange(steer_pieces(momentum, gradient)).reshape(count * rows, half)
    new_momentum = 0.95 * momentum + gradient.astype(jnp.float32)
    x, new_momentum = lax.optimization_barrier((x, new_momentum))
    own, sent = gram_half(x)
    other = partner(sent, "fsdp", 0)
    returned = exchange(update_half(x, own, other).reshape(count, rows, half))
    update = returned.reshape(mats, 2, rows, half).transpose(0, 2, 1, 3).reshape(mats, rows, width)
    return (new_momentum, update)


def solution(mesh):
    return jax.shard_map(
        local,
        mesh=mesh,
        in_specs=(P(None, "fsdp", None), P(None, "fsdp", None)),
        out_specs=(P(None, "fsdp", None), P(None, "fsdp", None)),
        check_vma=False,
    )
```

```python
import jax
import jax.numpy as jnp
from jax import lax
from jax.experimental import pallas as pl
from jax.experimental.pallas import tpu as pltpu
from jax.sharding import PartitionSpec as P

D = 3584
FF = 1024
ITERS = 3
LINEAR, CUBIC, QUINTIC = 3.4445, -4.775, 2.0315
FACTOR = 0.2 * max(FF, D) ** 0.5
TILE = 256
SIDE = FF // TILE
PAIRS = [(i, j) for j in range(SIDE) for i in range(j + 1)]
MIB = 2**20


def cost(flops, moved):
    return pl.CostEstimate(flops=flops, bytes_accessed=moved, transcendentals=0)


def span(i, size=TILE):
    return slice(i * size, (i + 1) * size)


def partner(x, axis, apart):
    return lax.ppermute(x, axis, [(i, i ^ 1 << apart) for i in range(lax.axis_size(axis))])


STEER_PARTS = 8


def steer_kernel(momentum, gradient, steer, m_buf, g_buf, s_buf, m_sem, g_sem, s_sem):
    mats, rows, width = m_buf.shape
    half = width // 2
    group = mats // STEER_PARTS
    arriving = []
    for c in range(STEER_PARTS):
        at = pl.ds(c * group, group)
        pair = (
            pltpu.make_async_copy(momentum.at[at], m_buf.at[at], m_sem.at[c]),
            pltpu.make_async_copy(gradient.at[at], g_buf.at[at], g_sem.at[c]),
        )
        for copy in pair:
            copy.start()
        arriving.append(pair)
    leaving = []
    for c in range(STEER_PARTS):
        for copy in arriving[c]:
            copy.wait()

        @pl.loop(c * group, (c + 1) * group)
        def _(m):
            g = g_buf[m].astype(jnp.float32)
            moved = 0.95 * m_buf[m] + g
            value = (g + 0.95 * moved).astype(jnp.bfloat16)
            s_buf[m, 0] = value[:, :half]
            s_buf[m, 1] = value[:, half:]

        at = pl.ds(c * group, group)
        copy = pltpu.make_async_copy(s_buf.at[at], steer.at[at], s_sem.at[c])
        copy.start()
        leaving.append(copy)
    for copy in leaving:
        copy.wait()


def steer_pieces(momentum, gradient):
    mats, rows, width = momentum.shape
    shape = (mats, 2, rows, width // 2)
    anywhere = pl.BlockSpec(memory_space=pl.ANY)
    dma = pltpu.SemaphoreType.DMA((STEER_PARTS,))
    return pl.pallas_call(
        steer_kernel,
        out_shape=jax.ShapeDtypeStruct(shape, jnp.bfloat16),
        in_specs=[anywhere] * 2,
        out_specs=anywhere,
        scratch_shapes=[
            pltpu.VMEM(momentum.shape, jnp.float32),
            pltpu.VMEM(gradient.shape, jnp.bfloat16),
            pltpu.VMEM(shape, jnp.bfloat16),
            dma,
            dma,
            dma,
        ],
        compiler_params=pltpu.CompilerParams(vmem_limit_bytes=56 * MIB),
        cost_estimate=cost(4 * momentum.size, 8 * momentum.size),
        name="steer",
    )(momentum, gradient).reshape(mats * 2, rows, width // 2)


def gram_kernel(x, own, sent):
    for j in reversed(range(SIDE)):
        value = lax.dot_general(
            x[0 : (j + 1) * TILE],
            x[span(j)],
            (((1,), (1,)), ((), ())),
            preferred_element_type=jnp.float32,
        )
        at = slice(j * (j + 1) // 2 * TILE, (j + 1) * (j + 2) // 2 * TILE)
        own[at] = value
        sent[at] = value.astype(jnp.bfloat16)


def gram_half(x):
    rows, part = x.shape
    shape = (len(PAIRS) * TILE, TILE)
    return pl.pallas_call(
        gram_kernel,
        out_shape=(
            jax.ShapeDtypeStruct(shape, jnp.float32),
            jax.ShapeDtypeStruct(shape, jnp.bfloat16),
        ),
        in_specs=[pl.BlockSpec(memory_space=pltpu.VMEM)],
        compiler_params=pltpu.CompilerParams(vmem_limit_bytes=16 * MIB),
        cost_estimate=cost(2 * len(PAIRS) * TILE * TILE * part, rows * part * 2 + len(PAIRS) * TILE * TILE * 6),
        name="gram",
    )(x)


def update_kernel(x, own, other, out, x_buf, g, h, s, w, m0, m1, x_sem):
    n, part = x_buf.shape
    loading = pltpu.make_async_copy(x, x_buf, x_sem)
    loading.start()
    here = lax.broadcasted_iota(jnp.int32, (TILE, TILE), 0) == lax.broadcasted_iota(
        jnp.int32, (TILE, TILE), 1
    )
    total = jnp.zeros((1, 1), jnp.float32)
    for k, (i, j) in enumerate(PAIRS):
        block = own[span(k)] + other[span(k)].astype(jnp.float32)
        narrow = block.astype(jnp.bfloat16)
        g[span(i), span(j)] = narrow
        if i == j:
            block = jnp.where(here, block, 0.0)
            block = jnp.sum(block, axis=0, keepdims=True)
            total = total + jnp.sum(block, axis=1, keepdims=True)
        else:
            g[span(j), span(i)] = narrow.T
    inverse = 1.0 / (jnp.sqrt(total) + 1e-07)
    factor = inverse * FACTOR
    square = inverse * inverse

    def product(left, right, store, rest):
        for j in reversed(range(SIDE)):
            at = (slice(0, (j + 1) * TILE), span(j))
            value = jnp.dot(left[at[0], :], right[:, at[1]], preferred_element_type=jnp.float32)
            narrow = rest(value, at).astype(jnp.bfloat16)
            store[at] = narrow
            for i in range(j):
                store[span(j), span(i)] = narrow[span(i)].T

    def wide(ref, at):
        return ref[at].astype(jnp.float32)


    product(g, g, m0, lambda v, at: square * (CUBIC * wide(g, at) + square * (QUINTIC * v)))
    product(m0, g, w, lambda v, at: square * (LINEAR * wide(g, at) + v))
    product(m0, w, h, lambda v, at: LINEAR * wide(w, at) + v)
    product(h, h, m1, lambda v, at: CUBIC * wide(h, at) + QUINTIC * v)
    product(m1, h, w, lambda v, at: LINEAR * wide(h, at) + v)
    product(m1, w, g, lambda v, at: LINEAR * wide(w, at) + v)
    product(m1, m0, s, lambda v, at: LINEAR * (wide(m0, at) + wide(m1, at)) + v)
    product(g, g, m0, lambda v, at: CUBIC * wide(g, at) + QUINTIC * v)
    product(m0, s, h, lambda v, at: LINEAR * wide(s, at) + LINEAR * LINEAR * wide(m0, at) + v)
    loading.wait()
    for i in range(SIDE):
        value = jnp.dot(h[span(i), :], x_buf[...], preferred_element_type=jnp.float32)
        value = value + LINEAR**3 * x_buf[span(i)].astype(jnp.float32)
        out[span(i)] = (value * factor).astype(jnp.bfloat16)


def update_half(x, own, other):
    n, part = x.shape
    anywhere = pl.BlockSpec(memory_space=pl.ANY)
    square = pltpu.VMEM((n, n), jnp.bfloat16)
    return pl.pallas_call(
        update_kernel,
        out_shape=jax.ShapeDtypeStruct((n, part), jnp.bfloat16),
        in_specs=[
            anywhere,
            pl.BlockSpec(memory_space=pltpu.VMEM),
            pl.BlockSpec(memory_space=pltpu.VMEM),
        ],
        out_specs=pl.BlockSpec(memory_space=pltpu.VMEM),
        scratch_shapes=[
            pltpu.VMEM((n, part), jnp.bfloat16),
            *[square] * 6,
            pltpu.SemaphoreType.DMA,
        ],
        compiler_params=pltpu.CompilerParams(vmem_limit_bytes=40 * MIB),
        cost_estimate=cost(2 * n * n * (9 * n + part), n * part * 4 + n * n * 6),
        name="update",
    )(x, own, other)


def exchange(x):
    return lax.all_to_all(x, "fsdp", split_axis=0, concat_axis=0, tiled=True)


def local(momentum, gradient):
    count = lax.axis_size("fsdp")
    mats, rows, width = momentum.shape
    half = width // 2
    x = exchange(steer_pieces(momentum, gradient)).reshape(count * rows, half)
    new_momentum = 0.95 * momentum + gradient.astype(jnp.float32)
    x, new_momentum = lax.optimization_barrier((x, new_momentum))
    own, sent = gram_half(x)
    other = partner(sent, "fsdp", 0)
    returned = exchange(update_half(x, own, other).reshape(count, rows, half))
    update = returned.reshape(mats, 2, rows, half).transpose(0, 2, 1, 3).reshape(mats, rows, width)
    return (new_momentum, update)


def solution(mesh):
    return jax.shard_map(
        local,
        mesh=mesh,
        in_specs=(P(None, "fsdp", None), P(None, "fsdp", None)),
        out_specs=(P(None, "fsdp", None), P(None, "fsdp", None)),
        check_vma=False,
    )
```

```python
import jax
import jax.numpy as jnp
from jax import lax
from jax.experimental import pallas as pl
from jax.experimental.pallas import tpu as pltpu
from jax.sharding import PartitionSpec as P

D = 3584
FF = 1024
ITERS = 3
LINEAR, CUBIC, QUINTIC = 3.4445, -4.775, 2.0315
FACTOR = 0.2 * max(FF, D) ** 0.5
TILE = 256
SIDE = FF // TILE
PAIRS = [(i, j) for j in range(SIDE) for i in range(j + 1)]
MIB = 2**20


def cost(flops, moved):
    return pl.CostEstimate(flops=flops, bytes_accessed=moved, transcendentals=0)


def span(i, size=TILE):
    return slice(i * size, (i + 1) * size)


def partner(x, axis, apart):
    return lax.ppermute(x, axis, [(i, i ^ 1 << apart) for i in range(lax.axis_size(axis))])


STEER_PARTS = 8
AFTER_PARTS = 4


def steer_kernel(momentum, gradient, *rest):
    afters, (steer, g_buf, m_sem, g_sem) = rest[:AFTER_PARTS], rest[AFTER_PARTS:]
    mats, rows, width = g_buf.shape
    half = width // 2
    group = mats // STEER_PARTS
    share = STEER_PARTS // AFTER_PARTS
    arriving = []
    for c in range(STEER_PARTS):
        at = pl.ds(c * group, group)
        after = afters[c // share].at[pl.ds(c % share * group, group)]
        pair = (
            pltpu.make_async_copy(momentum.at[at], after, m_sem.at[c]),
            pltpu.make_async_copy(gradient.at[at], g_buf.at[at], g_sem.at[c]),
        )
        for copy in pair:
            copy.start()
        arriving.append(pair)
    for c in range(STEER_PARTS):
        for copy in arriving[c]:
            copy.wait()

        after = afters[c // share]

        @pl.loop(0, group)
        def _(i):
            m = c * group + i
            place = c % share * group + i
            g = g_buf[m].astype(jnp.float32)
            moved = 0.95 * after[place] + g
            after[place] = moved
            value = (g + 0.95 * moved).astype(jnp.bfloat16)
            steer[m, 0] = value[:, :half]
            steer[m, 1] = value[:, half:]


def steer_pieces(momentum, gradient):
    mats, rows, width = momentum.shape
    shape = (mats, 2, rows, width // 2)
    anywhere = pl.BlockSpec(memory_space=pl.ANY)
    inside = pl.BlockSpec(memory_space=pltpu.VMEM)
    dma = pltpu.SemaphoreType.DMA((STEER_PARTS,))
    quarter = jax.ShapeDtypeStruct((mats // AFTER_PARTS, rows, width), jnp.float32)
    *afters, steer = pl.pallas_call(
        steer_kernel,
        out_shape=(
            *[quarter] * AFTER_PARTS,
            jax.ShapeDtypeStruct(shape, jnp.bfloat16),
        ),
        in_specs=[anywhere] * 2,
        out_specs=(inside,) * (AFTER_PARTS + 1),
        scratch_shapes=[pltpu.VMEM(gradient.shape, jnp.bfloat16), dma, dma],
        compiler_params=pltpu.CompilerParams(vmem_limit_bytes=40 * MIB),
        cost_estimate=cost(4 * momentum.size, 8 * momentum.size),
        name="steer",
    )(momentum, gradient)
    return afters, steer.reshape(mats * 2, rows, width // 2)


def gram_kernel(x, own, sent):
    for j in reversed(range(SIDE)):
        value = lax.dot_general(
            x[0 : (j + 1) * TILE],
            x[span(j)],
            (((1,), (1,)), ((), ())),
            preferred_element_type=jnp.float32,
        )
        at = slice(j * (j + 1) // 2 * TILE, (j + 1) * (j + 2) // 2 * TILE)
        own[at] = value
        sent[at] = value.astype(jnp.bfloat16)


def gram_half(x):
    rows, part = x.shape
    shape = (len(PAIRS) * TILE, TILE)
    return pl.pallas_call(
        gram_kernel,
        out_shape=(
            jax.ShapeDtypeStruct(shape, jnp.float32),
            jax.ShapeDtypeStruct(shape, jnp.bfloat16),
        ),
        in_specs=[pl.BlockSpec(memory_space=pltpu.VMEM)],
        compiler_params=pltpu.CompilerParams(vmem_limit_bytes=16 * MIB),
        cost_estimate=cost(2 * len(PAIRS) * TILE * TILE * part, rows * part * 2 + len(PAIRS) * TILE * TILE * 6),
        name="gram",
    )(x)


def update_kernel(x, own, other, *rest):
    afters = rest[:AFTER_PARTS]
    out, stored, x_buf, g, h, s, w, m0, m1, x_sem, after_sem = rest[AFTER_PARTS:]
    n, part = x_buf.shape
    loading = pltpu.make_async_copy(x, x_buf, x_sem)
    loading.start()
    storing = []
    for c, after in enumerate(afters):
        share = after.shape[0]
        copy = pltpu.make_async_copy(after, stored.at[pl.ds(c * share, share)], after_sem.at[c])
        copy.start()
        storing.append(copy)
    here = lax.broadcasted_iota(jnp.int32, (TILE, TILE), 0) == lax.broadcasted_iota(
        jnp.int32, (TILE, TILE), 1
    )
    total = jnp.zeros((1, 1), jnp.float32)
    for k, (i, j) in enumerate(PAIRS):
        block = own[span(k)] + other[span(k)].astype(jnp.float32)
        narrow = block.astype(jnp.bfloat16)
        g[span(i), span(j)] = narrow
        if i == j:
            block = jnp.where(here, block, 0.0)
            block = jnp.sum(block, axis=0, keepdims=True)
            total = total + jnp.sum(block, axis=1, keepdims=True)
        else:
            g[span(j), span(i)] = narrow.T
    inverse = 1.0 / (jnp.sqrt(total) + 1e-07)
    factor = inverse * FACTOR
    square = inverse * inverse

    def product(left, right, store, rest):
        for j in reversed(range(SIDE)):
            at = (slice(0, (j + 1) * TILE), span(j))
            value = jnp.dot(left[at[0], :], right[:, at[1]], preferred_element_type=jnp.float32)
            narrow = rest(value, at).astype(jnp.bfloat16)
            store[at] = narrow
            for i in range(j):
                store[span(j), span(i)] = narrow[span(i)].T

    def wide(ref, at):
        return ref[at].astype(jnp.float32)


    product(g, g, m0, lambda v, at: square * (CUBIC * wide(g, at) + square * (QUINTIC * v)))
    product(m0, g, w, lambda v, at: square * (LINEAR * wide(g, at) + v))
    product(m0, w, h, lambda v, at: LINEAR * wide(w, at) + v)
    product(h, h, m1, lambda v, at: CUBIC * wide(h, at) + QUINTIC * v)
    product(m1, h, w, lambda v, at: LINEAR * wide(h, at) + v)
    product(m1, w, g, lambda v, at: LINEAR * wide(w, at) + v)
    product(m1, m0, s, lambda v, at: LINEAR * (wide(m0, at) + wide(m1, at)) + v)
    product(g, g, m0, lambda v, at: CUBIC * wide(g, at) + QUINTIC * v)
    product(m0, s, h, lambda v, at: LINEAR * wide(s, at) + LINEAR * LINEAR * wide(m0, at) + v)
    loading.wait()
    for i in range(SIDE):
        value = jnp.dot(h[span(i), :], x_buf[...], preferred_element_type=jnp.float32)
        value = value + LINEAR**3 * x_buf[span(i)].astype(jnp.float32)
        out[span(i)] = (value * factor).astype(jnp.bfloat16)
    for copy in storing:
        copy.wait()


def update_half(x, own, other, afters):
    n, part = x.shape
    anywhere = pl.BlockSpec(memory_space=pl.ANY)
    inside = pl.BlockSpec(memory_space=pltpu.VMEM)
    square = pltpu.VMEM((n, n), jnp.bfloat16)
    return pl.pallas_call(
        update_kernel,
        out_shape=(
            jax.ShapeDtypeStruct((n, part), jnp.bfloat16),
            jax.ShapeDtypeStruct((afters[0].shape[0] * AFTER_PARTS, *afters[0].shape[1:]), jnp.float32),
        ),
        in_specs=[anywhere, inside, inside, *[anywhere] * AFTER_PARTS],
        out_specs=(inside, anywhere),
        scratch_shapes=[
            pltpu.VMEM((n, part), jnp.bfloat16),
            *[square] * 6,
            pltpu.SemaphoreType.DMA,
            pltpu.SemaphoreType.DMA((AFTER_PARTS,)),
        ],
        compiler_params=pltpu.CompilerParams(vmem_limit_bytes=30 * MIB),
        cost_estimate=cost(2 * n * n * (9 * n + part), n * part * 4 + n * n * 6),
        name="update",
    )(x, own, other, *afters)


def exchange(x):
    return lax.all_to_all(x, "fsdp", split_axis=0, concat_axis=0, tiled=True)


def local(momentum, gradient):
    count = lax.axis_size("fsdp")
    mats, rows, width = momentum.shape
    half = width // 2
    afters, pieces = steer_pieces(momentum, gradient)
    x = exchange(pieces).reshape(count * rows, half)
    own, sent = gram_half(x)
    other = partner(sent, "fsdp", 0)
    outgoing, new_momentum = update_half(x, own, other, afters)
    returned = exchange(outgoing.reshape(count, rows, half))
    update = returned.reshape(mats, 2, rows, half).transpose(0, 2, 1, 3).reshape(mats, rows, width)
    return (new_momentum, update)


def solution(mesh):
    return jax.shard_map(
        local,
        mesh=mesh,
        in_specs=(P(None, "fsdp", None), P(None, "fsdp", None)),
        out_specs=(P(None, "fsdp", None), P(None, "fsdp", None)),
        check_vma=False,
    )
```

```python
import jax
import jax.numpy as jnp
from jax import lax
from jax.experimental import pallas as pl
from jax.experimental.pallas import tpu as pltpu
from jax.sharding import PartitionSpec as P

D = 3584
FF = 1024
ITERS = 3
LINEAR, CUBIC, QUINTIC = 3.4445, -4.775, 2.0315
FACTOR = 0.2 * max(FF, D) ** 0.5
TILE = 256
SIDE = FF // TILE
PAIRS = [(i, j) for j in range(SIDE) for i in range(j + 1)]
MIB = 2**20


def cost(flops, moved):
    return pl.CostEstimate(flops=flops, bytes_accessed=moved, transcendentals=0)


def span(i, size=TILE):
    return slice(i * size, (i + 1) * size)


def partner(x, axis, apart):
    return lax.ppermute(x, axis, [(i, i ^ 1 << apart) for i in range(lax.axis_size(axis))])


STEER_PARTS = 8
AFTER_PARTS = 4


def steer_kernel(momentum, gradient, *rest):
    afters, (steer, g_buf, m_sem, g_sem) = rest[:AFTER_PARTS], rest[AFTER_PARTS:]
    mats, rows, width = g_buf.shape
    half = width // 2
    group = mats // STEER_PARTS
    share = STEER_PARTS // AFTER_PARTS
    arriving = []
    for c in range(STEER_PARTS):
        at = pl.ds(c * group, group)
        after = afters[c // share].at[pl.ds(c % share * group, group)]
        pair = (
            pltpu.make_async_copy(momentum.at[at], after, m_sem.at[c]),
            pltpu.make_async_copy(gradient.at[at], g_buf.at[at], g_sem.at[c]),
        )
        for copy in pair:
            copy.start()
        arriving.append(pair)
    for c in range(STEER_PARTS):
        for copy in arriving[c]:
            copy.wait()

        after = afters[c // share]

        @pl.loop(0, group)
        def _(i):
            m = c * group + i
            place = c % share * group + i
            g = g_buf[m].astype(jnp.float32)
            moved = 0.95 * after[place] + g
            after[place] = moved
            value = (g + 0.95 * moved).astype(jnp.bfloat16)
            steer[m, 0] = value[:, :half]
            steer[m, 1] = value[:, half:]


def steer_pieces(momentum, gradient):
    mats, rows, width = momentum.shape
    shape = (mats, 2, rows, width // 2)
    anywhere = pl.BlockSpec(memory_space=pl.ANY)
    inside = pl.BlockSpec(memory_space=pltpu.VMEM)
    dma = pltpu.SemaphoreType.DMA((STEER_PARTS,))
    quarter = jax.ShapeDtypeStruct((mats // AFTER_PARTS, rows, width), jnp.float32)
    *afters, steer = pl.pallas_call(
        steer_kernel,
        out_shape=(
            *[quarter] * AFTER_PARTS,
            jax.ShapeDtypeStruct(shape, jnp.bfloat16),
        ),
        in_specs=[anywhere] * 2,
        out_specs=(inside,) * (AFTER_PARTS + 1),
        scratch_shapes=[pltpu.VMEM(gradient.shape, jnp.bfloat16), dma, dma],
        compiler_params=pltpu.CompilerParams(vmem_limit_bytes=40 * MIB),
        cost_estimate=cost(4 * momentum.size, 8 * momentum.size),
        name="steer",
    )(momentum, gradient)
    return afters, steer.reshape(mats * 2, rows, width // 2)


def gram_kernel(x, own, sent):
    for j in reversed(range(SIDE)):
        value = lax.dot_general(
            x[0 : (j + 1) * TILE],
            x[span(j)],
            (((1,), (1,)), ((), ())),
            preferred_element_type=jnp.float32,
        )
        at = slice(j * (j + 1) // 2 * TILE, (j + 1) * (j + 2) // 2 * TILE)
        own[at] = value
        sent[at] = value.astype(jnp.bfloat16)


def gram_half(x):
    rows, part = x.shape
    shape = (len(PAIRS) * TILE, TILE)
    return pl.pallas_call(
        gram_kernel,
        out_shape=(
            jax.ShapeDtypeStruct(shape, jnp.float32),
            jax.ShapeDtypeStruct(shape, jnp.bfloat16),
        ),
        in_specs=[pl.BlockSpec(memory_space=pltpu.VMEM)],
        compiler_params=pltpu.CompilerParams(vmem_limit_bytes=16 * MIB),
        cost_estimate=cost(2 * len(PAIRS) * TILE * TILE * part, rows * part * 2 + len(PAIRS) * TILE * TILE * 6),
        name="gram",
    )(x)


def update_kernel(x, own, other, *rest):
    afters = rest[:AFTER_PARTS]
    out, stored, g, h, s, w, m0, m1, after_sem = rest[AFTER_PARTS:]
    storing = []
    for c, after in enumerate(afters):
        share = after.shape[0]
        copy = pltpu.make_async_copy(after, stored.at[pl.ds(c * share, share)], after_sem.at[c])
        copy.start()
        storing.append(copy)
    here = lax.broadcasted_iota(jnp.int32, (TILE, TILE), 0) == lax.broadcasted_iota(
        jnp.int32, (TILE, TILE), 1
    )
    total = jnp.zeros((1, 1), jnp.float32)
    for k, (i, j) in enumerate(PAIRS):
        block = own[span(k)] + other[span(k)].astype(jnp.float32)
        narrow = block.astype(jnp.bfloat16)
        g[span(i), span(j)] = narrow
        if i == j:
            block = jnp.where(here, block, 0.0)
            block = jnp.sum(block, axis=0, keepdims=True)
            total = total + jnp.sum(block, axis=1, keepdims=True)
        else:
            g[span(j), span(i)] = narrow.T
    inverse = 1.0 / (jnp.sqrt(total) + 1e-07)
    factor = inverse * FACTOR
    direct = LINEAR**3 * factor
    square = inverse * inverse

    def product(left, right, store, rest):
        for j in reversed(range(SIDE)):
            at = (slice(0, (j + 1) * TILE), span(j))
            value = jnp.dot(left[at[0], :], right[:, at[1]], preferred_element_type=jnp.float32)
            narrow = rest(value, at).astype(jnp.bfloat16)
            store[at] = narrow
            for i in range(j):
                store[span(j), span(i)] = narrow[span(i)].T

    def wide(ref, at):
        return ref[at].astype(jnp.float32)


    product(g, g, m0, lambda v, at: square * (CUBIC * wide(g, at) + square * (QUINTIC * v)))
    product(m0, g, w, lambda v, at: square * (LINEAR * wide(g, at) + v))
    product(m0, w, h, lambda v, at: LINEAR * wide(w, at) + v)
    product(h, h, m1, lambda v, at: CUBIC * wide(h, at) + QUINTIC * v)
    product(m1, h, w, lambda v, at: LINEAR * wide(h, at) + v)
    product(m1, w, g, lambda v, at: LINEAR * wide(w, at) + v)
    product(m1, m0, s, lambda v, at: LINEAR * (wide(m0, at) + wide(m1, at)) + v)
    product(g, g, m0, lambda v, at: CUBIC * wide(g, at) + QUINTIC * v)
    product(
        m0, s, h, lambda v, at: factor * (LINEAR * wide(s, at) + LINEAR * LINEAR * wide(m0, at) + v)
    )
    for i in reversed(range(SIDE)):
        value = jnp.dot(h[span(i), :], x[...], preferred_element_type=jnp.float32)
        out[span(i)] = (value + direct * x[span(i)].astype(jnp.float32)).astype(jnp.bfloat16)
    for copy in storing:
        copy.wait()


def update_half(x, own, other, afters):
    n, part = x.shape
    anywhere = pl.BlockSpec(memory_space=pl.ANY)
    inside = pl.BlockSpec(memory_space=pltpu.VMEM)
    square = pltpu.VMEM((n, n), jnp.bfloat16)
    return pl.pallas_call(
        update_kernel,
        out_shape=(
            jax.ShapeDtypeStruct((n, part), jnp.bfloat16),
            jax.ShapeDtypeStruct((afters[0].shape[0] * AFTER_PARTS, *afters[0].shape[1:]), jnp.float32),
        ),
        in_specs=[inside, inside, inside, *[anywhere] * AFTER_PARTS],
        out_specs=(inside, anywhere),
        scratch_shapes=[
            *[square] * 6,
            pltpu.SemaphoreType.DMA((AFTER_PARTS,)),
        ],
        compiler_params=pltpu.CompilerParams(vmem_limit_bytes=30 * MIB),
        cost_estimate=cost(2 * n * n * (9 * n + part), n * part * 4 + n * n * 6),
        name="update",
    )(x, own, other, *afters)


def exchange(x):
    return lax.all_to_all(x, "fsdp", split_axis=0, concat_axis=0, tiled=True)


def local(momentum, gradient):
    count = lax.axis_size("fsdp")
    mats, rows, width = momentum.shape
    half = width // 2
    afters, pieces = steer_pieces(momentum, gradient)
    x = exchange(pieces).reshape(count * rows, half)
    own, sent = gram_half(x)
    other = partner(sent, "fsdp", 0)
    outgoing, new_momentum = update_half(x, own, other, afters)
    returned = exchange(outgoing.reshape(count, rows, half))
    update = returned.reshape(mats, 2, rows, half).transpose(0, 2, 1, 3).reshape(mats, rows, width)
    return (new_momentum, update)


def solution(mesh):
    return jax.shard_map(
        local,
        mesh=mesh,
        in_specs=(P(None, "fsdp", None), P(None, "fsdp", None)),
        out_specs=(P(None, "fsdp", None), P(None, "fsdp", None)),
        check_vma=False,
    )
```

```python
import functools

import jax
import jax.numpy as jnp
from jax import lax
from jax.experimental import pallas as pl
from jax.experimental.pallas import tpu as pltpu
from jax.sharding import PartitionSpec as P

D = 3584
FF = 1024
ITERS = 3
LINEAR, CUBIC, QUINTIC = 3.4445, -4.775, 2.0315
FACTOR = 0.2 * max(FF, D) ** 0.5
TILE = 256
SIDE = FF // TILE
GROUPS = [(2, 1, 0), (3,)]
PAIRS = [[(i, j) for j in group for i in range(j + 1)] for group in GROUPS]
MIB = 2**20


def cost(flops, moved):
    return pl.CostEstimate(flops=flops, bytes_accessed=moved, transcendentals=0)


def span(i, size=TILE):
    return slice(i * size, (i + 1) * size)


def partner(x, axis, apart):
    return lax.ppermute(x, axis, [(i, i ^ 1 << apart) for i in range(lax.axis_size(axis))])


STEER_PARTS = 8
AFTER_PARTS = 4


def steer_kernel(momentum, gradient, *rest):
    afters, (steer, g_buf, m_sem, g_sem) = rest[:AFTER_PARTS], rest[AFTER_PARTS:]
    mats, rows, width = g_buf.shape
    half = width // 2
    group = mats // STEER_PARTS
    share = STEER_PARTS // AFTER_PARTS
    arriving = []
    for c in range(STEER_PARTS):
        at = pl.ds(c * group, group)
        after = afters[c // share].at[pl.ds(c % share * group, group)]
        pair = (
            pltpu.make_async_copy(momentum.at[at], after, m_sem.at[c]),
            pltpu.make_async_copy(gradient.at[at], g_buf.at[at], g_sem.at[c]),
        )
        for copy in pair:
            copy.start()
        arriving.append(pair)
    for c in range(STEER_PARTS):
        for copy in arriving[c]:
            copy.wait()

        after = afters[c // share]

        @pl.loop(0, group)
        def _(i):
            m = c * group + i
            place = c % share * group + i
            g = g_buf[m].astype(jnp.float32)
            moved = 0.95 * after[place] + g
            after[place] = moved
            value = (g + 0.95 * moved).astype(jnp.bfloat16)
            steer[m, 0] = value[:, :half]
            steer[m, 1] = value[:, half:]


def steer_pieces(momentum, gradient):
    mats, rows, width = momentum.shape
    shape = (mats, 2, rows, width // 2)
    anywhere = pl.BlockSpec(memory_space=pl.ANY)
    inside = pl.BlockSpec(memory_space=pltpu.VMEM)
    dma = pltpu.SemaphoreType.DMA((STEER_PARTS,))
    quarter = jax.ShapeDtypeStruct((mats // AFTER_PARTS, rows, width), jnp.float32)
    *afters, steer = pl.pallas_call(
        steer_kernel,
        out_shape=(
            *[quarter] * AFTER_PARTS,
            jax.ShapeDtypeStruct(shape, jnp.bfloat16),
        ),
        in_specs=[anywhere] * 2,
        out_specs=(inside,) * (AFTER_PARTS + 1),
        scratch_shapes=[pltpu.VMEM(gradient.shape, jnp.bfloat16), dma, dma],
        compiler_params=pltpu.CompilerParams(vmem_limit_bytes=40 * MIB),
        cost_estimate=cost(4 * momentum.size, 8 * momentum.size),
        name="steer",
    )(momentum, gradient)
    return afters, steer.reshape(mats * 2, rows, width // 2)


def gram_kernel(group, x, own, sent):
    start = 0
    for j in group:
        value = lax.dot_general(
            x[0 : (j + 1) * TILE],
            x[span(j)],
            (((1,), (1,)), ((), ())),
            preferred_element_type=jnp.float32,
        )
        at = slice(start, start + (j + 1) * TILE)
        start += (j + 1) * TILE
        own[at] = value
        sent[at] = value.astype(jnp.bfloat16)


def gram_half(x, group, pairs):
    rows, part = x.shape
    shape = (len(pairs) * TILE, TILE)
    return pl.pallas_call(
        functools.partial(gram_kernel, group),
        out_shape=(
            jax.ShapeDtypeStruct(shape, jnp.float32),
            jax.ShapeDtypeStruct(shape, jnp.bfloat16),
        ),
        in_specs=[pl.BlockSpec(memory_space=pltpu.VMEM)],
        compiler_params=pltpu.CompilerParams(vmem_limit_bytes=16 * MIB),
        cost_estimate=cost(2 * len(pairs) * TILE * TILE * part, rows * part * 2 + len(pairs) * TILE * TILE * 6),
        name="gram",
    )(x)


def update_kernel(x, *rest):
    owns, others, rest = rest[: len(GROUPS)], rest[len(GROUPS) : 2 * len(GROUPS)], rest[2 * len(GROUPS) :]
    afters = rest[:AFTER_PARTS]
    out, stored, g, h, s, w, m0, m1, after_sem = rest[AFTER_PARTS:]
    storing = []
    for c, after in enumerate(afters):
        share = after.shape[0]
        copy = pltpu.make_async_copy(after, stored.at[pl.ds(c * share, share)], after_sem.at[c])
        copy.start()
        storing.append(copy)
    here = lax.broadcasted_iota(jnp.int32, (TILE, TILE), 0) == lax.broadcasted_iota(
        jnp.int32, (TILE, TILE), 1
    )
    total = jnp.zeros((1, 1), jnp.float32)
    for own, other, pairs in zip(owns, others, PAIRS):
        for k, (i, j) in enumerate(pairs):
            block = own[span(k)] + other[span(k)].astype(jnp.float32)
            narrow = block.astype(jnp.bfloat16)
            g[span(i), span(j)] = narrow
            if i == j:
                block = jnp.where(here, block, 0.0)
                block = jnp.sum(block, axis=0, keepdims=True)
                total = total + jnp.sum(block, axis=1, keepdims=True)
            else:
                g[span(j), span(i)] = narrow.T
    inverse = 1.0 / (jnp.sqrt(total) + 1e-07)
    factor = inverse * FACTOR
    direct = LINEAR**3 * factor
    square = inverse * inverse

    def product(left, right, store, rest):
        for j in reversed(range(SIDE)):
            at = (slice(0, (j + 1) * TILE), span(j))
            value = jnp.dot(left[at[0], :], right[:, at[1]], preferred_element_type=jnp.float32)
            narrow = rest(value, at).astype(jnp.bfloat16)
            store[at] = narrow
            for i in range(j):
                store[span(j), span(i)] = narrow[span(i)].T

    def wide(ref, at):
        return ref[at].astype(jnp.float32)


    product(g, g, m0, lambda v, at: square * (CUBIC * wide(g, at) + square * (QUINTIC * v)))
    product(m0, g, w, lambda v, at: square * (LINEAR * wide(g, at) + v))
    product(m0, w, h, lambda v, at: LINEAR * wide(w, at) + v)
    product(h, h, m1, lambda v, at: CUBIC * wide(h, at) + QUINTIC * v)
    product(m1, h, w, lambda v, at: LINEAR * wide(h, at) + v)
    product(m1, w, g, lambda v, at: LINEAR * wide(w, at) + v)
    product(m1, m0, s, lambda v, at: LINEAR * (wide(m0, at) + wide(m1, at)) + v)
    product(g, g, m0, lambda v, at: CUBIC * wide(g, at) + QUINTIC * v)
    product(
        m0, s, h, lambda v, at: factor * (LINEAR * wide(s, at) + LINEAR * LINEAR * wide(m0, at) + v)
    )
    for i in reversed(range(SIDE)):
        value = jnp.dot(h[span(i), :], x[...], preferred_element_type=jnp.float32)
        out[span(i)] = (value + direct * x[span(i)].astype(jnp.float32)).astype(jnp.bfloat16)
    for copy in storing:
        copy.wait()


def update_half(x, owns, others, afters):
    n, part = x.shape
    anywhere = pl.BlockSpec(memory_space=pl.ANY)
    inside = pl.BlockSpec(memory_space=pltpu.VMEM)
    square = pltpu.VMEM((n, n), jnp.bfloat16)
    return pl.pallas_call(
        update_kernel,
        out_shape=(
            jax.ShapeDtypeStruct((n, part), jnp.bfloat16),
            jax.ShapeDtypeStruct((afters[0].shape[0] * AFTER_PARTS, *afters[0].shape[1:]), jnp.float32),
        ),
        in_specs=[inside, *[inside] * (2 * len(GROUPS)), *[anywhere] * AFTER_PARTS],
        out_specs=(inside, anywhere),
        scratch_shapes=[
            *[square] * 6,
            pltpu.SemaphoreType.DMA((AFTER_PARTS,)),
        ],
        compiler_params=pltpu.CompilerParams(vmem_limit_bytes=30 * MIB),
        cost_estimate=cost(2 * n * n * (9 * n + part), n * part * 4 + n * n * 6),
        name="update",
    )(x, *owns, *others, *afters)


def exchange(x):
    return lax.all_to_all(x, "fsdp", split_axis=0, concat_axis=0, tiled=True)


def local(momentum, gradient):
    count = lax.axis_size("fsdp")
    mats, rows, width = momentum.shape
    half = width // 2
    afters, pieces = steer_pieces(momentum, gradient)
    x = exchange(pieces).reshape(count * rows, half)
    owns, others = [], []
    for group, pairs in zip(GROUPS, PAIRS):
        own, sent = gram_half(x, group, pairs)
        owns.append(own)
        others.append(partner(sent, "fsdp", 0))
    outgoing, new_momentum = update_half(x, owns, others, afters)
    returned = exchange(outgoing.reshape(count, rows, half))
    update = returned.reshape(mats, 2, rows, half).transpose(0, 2, 1, 3).reshape(mats, rows, width)
    return (new_momentum, update)


def solution(mesh):
    return jax.shard_map(
        local,
        mesh=mesh,
        in_specs=(P(None, "fsdp", None), P(None, "fsdp", None)),
        out_specs=(P(None, "fsdp", None), P(None, "fsdp", None)),
        check_vma=False,
    )
```

```python
import functools

import jax
import jax.numpy as jnp
from jax import lax
from jax.experimental import pallas as pl
from jax.experimental.pallas import tpu as pltpu
from jax.sharding import PartitionSpec as P

D = 3584
FF = 1024
ITERS = 3
LINEAR, CUBIC, QUINTIC = 3.4445, -4.775, 2.0315
FACTOR = 0.2 * max(FF, D) ** 0.5
TILE = 256
SIDE = FF // TILE
GROUPS = [(2, 1, 0), (3,)]
PAIRS = [[(i, j) for j in group for i in range(j + 1)] for group in GROUPS]
MIB = 2**20


def cost(flops, moved):
    return pl.CostEstimate(flops=flops, bytes_accessed=moved, transcendentals=0)


def span(i, size=TILE):
    return slice(i * size, (i + 1) * size)


def partner(x, axis, apart):
    return lax.ppermute(x, axis, [(i, i ^ 1 << apart) for i in range(lax.axis_size(axis))])


STEER_PARTS = 8
AFTER_PARTS = 4


def steer_kernel(momentum, gradient, *rest):
    afters, (steer, g_buf, m_sem, g_sem) = rest[:AFTER_PARTS], rest[AFTER_PARTS:]
    mats, rows, width = g_buf.shape
    half = width // 2
    group = mats // STEER_PARTS
    share = STEER_PARTS // AFTER_PARTS
    arriving = []
    for c in range(STEER_PARTS):
        at = pl.ds(c * group, group)
        after = afters[c // share].at[pl.ds(c % share * group, group)]
        pair = (
            pltpu.make_async_copy(momentum.at[at], after, m_sem.at[c]),
            pltpu.make_async_copy(gradient.at[at], g_buf.at[at], g_sem.at[c]),
        )
        for copy in pair:
            copy.start()
        arriving.append(pair)
    for c in range(STEER_PARTS):
        for copy in arriving[c]:
            copy.wait()

        after = afters[c // share]

        @pl.loop(0, group)
        def _(i):
            m = c * group + i
            place = c % share * group + i
            g = g_buf[m].astype(jnp.float32)
            moved = 0.95 * after[place] + g
            after[place] = moved
            value = (g + 0.95 * moved).astype(jnp.bfloat16)
            steer[m, 0] = value[:, :half]
            steer[m, 1] = value[:, half:]


def steer_pieces(momentum, gradient):
    mats, rows, width = momentum.shape
    shape = (mats, 2, rows, width // 2)
    anywhere = pl.BlockSpec(memory_space=pl.ANY)
    inside = pl.BlockSpec(memory_space=pltpu.VMEM)
    dma = pltpu.SemaphoreType.DMA((STEER_PARTS,))
    quarter = jax.ShapeDtypeStruct((mats // AFTER_PARTS, rows, width), jnp.float32)
    *afters, steer = pl.pallas_call(
        steer_kernel,
        out_shape=(
            *[quarter] * AFTER_PARTS,
            jax.ShapeDtypeStruct(shape, jnp.bfloat16),
        ),
        in_specs=[anywhere] * 2,
        out_specs=(inside,) * (AFTER_PARTS + 1),
        scratch_shapes=[pltpu.VMEM(gradient.shape, jnp.bfloat16), dma, dma],
        compiler_params=pltpu.CompilerParams(vmem_limit_bytes=40 * MIB),
        cost_estimate=cost(4 * momentum.size, 8 * momentum.size),
        name="steer",
    )(momentum, gradient)
    return afters, steer.reshape(mats * 2, rows, width // 2)


def gram_kernel(group, x, own, sent):
    start = 0
    for j in group:
        value = lax.dot_general(
            x[0 : (j + 1) * TILE],
            x[span(j)],
            (((1,), (1,)), ((), ())),
            preferred_element_type=jnp.float32,
        )
        at = slice(start, start + (j + 1) * TILE)
        start += (j + 1) * TILE
        own[at] = value
        sent[at] = value.astype(jnp.bfloat16)


def gram_half(x, group, pairs):
    rows, part = x.shape
    shape = (len(pairs) * TILE, TILE)
    return pl.pallas_call(
        functools.partial(gram_kernel, group),
        out_shape=(
            jax.ShapeDtypeStruct(shape, jnp.float32),
            jax.ShapeDtypeStruct(shape, jnp.bfloat16),
        ),
        in_specs=[pl.BlockSpec(memory_space=pltpu.VMEM)],
        compiler_params=pltpu.CompilerParams(vmem_limit_bytes=16 * MIB),
        cost_estimate=cost(2 * len(pairs) * TILE * TILE * part, rows * part * 2 + len(pairs) * TILE * TILE * 6),
        name="gram",
    )(x)


def update_kernel(x, *rest):
    owns, others, rest = rest[: len(GROUPS)], rest[len(GROUPS) : 2 * len(GROUPS)], rest[2 * len(GROUPS) :]
    afters = rest[:AFTER_PARTS]
    out, stored, g, h, s, w, m0, m1, after_sem = rest[AFTER_PARTS:]
    storing = []
    for c, after in enumerate(afters):
        share = after.shape[0]
        copy = pltpu.make_async_copy(after, stored.at[pl.ds(c * share, share)], after_sem.at[c])
        copy.start()
        storing.append(copy)
    here = lax.broadcasted_iota(jnp.int32, (TILE, TILE), 0) == lax.broadcasted_iota(
        jnp.int32, (TILE, TILE), 1
    )
    total = jnp.zeros((1, 1), jnp.float32)
    for own, other, pairs in zip(owns, others, PAIRS):
        for k, (i, j) in enumerate(pairs):
            block = own[span(k)] + other[span(k)].astype(jnp.float32)
            narrow = block.astype(jnp.bfloat16)
            g[span(i), span(j)] = narrow
            if i == j:
                block = jnp.where(here, block, 0.0)
                block = jnp.sum(block, axis=0, keepdims=True)
                total = total + jnp.sum(block, axis=1, keepdims=True)
            else:
                g[span(j), span(i)] = narrow.T
    inverse = 1.0 / (jnp.sqrt(total) + 1e-07)
    factor = inverse * FACTOR
    direct = LINEAR**3 * factor
    square = inverse * inverse

    def product(left, right, store, rest):
        lost = [None] * SIDE
        for j in reversed(range(SIDE)):
            at = (slice(0, (j + 1) * TILE), span(j))
            value = jnp.dot(left[at[0], :], right[:, at[1]], preferred_element_type=jnp.float32)
            value = rest(value, at, j)
            narrow = value.astype(jnp.bfloat16)
            store[at] = narrow
            for i in range(j):
                store[span(j), span(i)] = narrow[span(i)].T
            lost[j] = jnp.where(here, value[span(j)] - narrow[span(j)].astype(jnp.float32), 0.0)
        return lost

    def wide(ref, at):
        return ref[at].astype(jnp.float32)


    product(g, g, m0, lambda v, at, j: square * (CUBIC * wide(g, at) + square * (QUINTIC * v)))
    product(m0, g, w, lambda v, at, j: square * (LINEAR * wide(g, at) + v))
    product(m0, w, h, lambda v, at, j: LINEAR * wide(w, at) + v)
    product(h, h, m1, lambda v, at, j: CUBIC * wide(h, at) + QUINTIC * v)
    product(m1, h, w, lambda v, at, j: LINEAR * wide(h, at) + v)
    product(m1, w, g, lambda v, at, j: LINEAR * wide(w, at) + v)
    lost = product(m1, m0, s, lambda v, at, j: LINEAR * (wide(m0, at) + wide(m1, at)) + v)
    across = [jnp.sum(block, axis=0, keepdims=True) for block in lost]
    down = [LINEAR * jnp.sum(block, axis=1, keepdims=True) for block in lost]
    product(g, g, m0, lambda v, at, j: CUBIC * wide(g, at) + QUINTIC * v)
    lost = product(
        m0,
        s,
        h,
        lambda v, at, j: factor
        * (LINEAR * wide(s, at) + (LINEAR * LINEAR + across[j]) * wide(m0, at) + v),
    )
    for i in reversed(range(SIDE)):
        value = jnp.dot(h[span(i), :], x[...], preferred_element_type=jnp.float32)
        diagonal = direct + factor * down[i] + jnp.sum(lost[i], axis=1, keepdims=True)
        out[span(i)] = (value + diagonal * x[span(i)].astype(jnp.float32)).astype(jnp.bfloat16)
    for copy in storing:
        copy.wait()


def update_half(x, owns, others, afters):
    n, part = x.shape
    anywhere = pl.BlockSpec(memory_space=pl.ANY)
    inside = pl.BlockSpec(memory_space=pltpu.VMEM)
    square = pltpu.VMEM((n, n), jnp.bfloat16)
    return pl.pallas_call(
        update_kernel,
        out_shape=(
            jax.ShapeDtypeStruct((n, part), jnp.bfloat16),
            jax.ShapeDtypeStruct((afters[0].shape[0] * AFTER_PARTS, *afters[0].shape[1:]), jnp.float32),
        ),
        in_specs=[inside, *[inside] * (2 * len(GROUPS)), *[anywhere] * AFTER_PARTS],
        out_specs=(inside, anywhere),
        scratch_shapes=[
            *[square] * 6,
            pltpu.SemaphoreType.DMA((AFTER_PARTS,)),
        ],
        compiler_params=pltpu.CompilerParams(vmem_limit_bytes=30 * MIB),
        cost_estimate=cost(2 * n * n * (9 * n + part), n * part * 4 + n * n * 6),
        name="update",
    )(x, *owns, *others, *afters)


def exchange(x):
    return lax.all_to_all(x, "fsdp", split_axis=0, concat_axis=0, tiled=True)


def local(momentum, gradient):
    count = lax.axis_size("fsdp")
    mats, rows, width = momentum.shape
    half = width // 2
    afters, pieces = steer_pieces(momentum, gradient)
    x = exchange(pieces).reshape(count * rows, half)
    owns, others = [], []
    for group, pairs in zip(GROUPS, PAIRS):
        own, sent = gram_half(x, group, pairs)
        owns.append(own)
        others.append(partner(sent, "fsdp", 0))
    outgoing, new_momentum = update_half(x, owns, others, afters)
    returned = exchange(outgoing.reshape(count, rows, half))
    update = returned.reshape(mats, 2, rows, half).transpose(0, 2, 1, 3).reshape(mats, rows, width)
    return (new_momentum, update)


def solution(mesh):
    return jax.shard_map(
        local,
        mesh=mesh,
        in_specs=(P(None, "fsdp", None), P(None, "fsdp", None)),
        out_specs=(P(None, "fsdp", None), P(None, "fsdp", None)),
        check_vma=False,
    )
```

```python
import functools

import jax
import jax.numpy as jnp
from jax import lax
from jax.experimental import pallas as pl
from jax.experimental.pallas import tpu as pltpu
from jax.sharding import PartitionSpec as P

D = 3584
FF = 1024
ITERS = 3
LINEAR, CUBIC, QUINTIC = 3.4445, -4.775, 2.0315
FACTOR = 0.2 * max(FF, D) ** 0.5
TILE = 256
SIDE = FF // TILE
GROUPS = [(2, 1, 0), (3,)]
PAIRS = [[(i, j) for j in group for i in range(j + 1)] for group in GROUPS]
MIB = 2**20


def cost(flops, moved):
    return pl.CostEstimate(flops=flops, bytes_accessed=moved, transcendentals=0)


def span(i, size=TILE):
    return slice(i * size, (i + 1) * size)


def partner(x, axis, apart):
    return lax.ppermute(x, axis, [(i, i ^ 1 << apart) for i in range(lax.axis_size(axis))])


STEER_PARTS = 8
AFTER_PARTS = 4


def steer_kernel(momentum, gradient, *rest):
    afters, (steer, g_buf, m_sem, g_sem) = rest[:AFTER_PARTS], rest[AFTER_PARTS:]
    mats, rows, width = g_buf.shape
    half = width // 2
    group = mats // STEER_PARTS
    share = STEER_PARTS // AFTER_PARTS
    arriving = []
    for c in range(STEER_PARTS):
        at = pl.ds(c * group, group)
        after = afters[c // share].at[pl.ds(c % share * group, group)]
        pair = (
            pltpu.make_async_copy(momentum.at[at], after, m_sem.at[c]),
            pltpu.make_async_copy(gradient.at[at], g_buf.at[at], g_sem.at[c]),
        )
        for copy in pair:
            copy.start()
        arriving.append(pair)
    for c in range(STEER_PARTS):
        for copy in arriving[c]:
            copy.wait()

        after = afters[c // share]

        @pl.loop(0, group)
        def _(i):
            m = c * group + i
            place = c % share * group + i
            g = g_buf[m].astype(jnp.float32)
            moved = 0.95 * after[place] + g
            after[place] = moved
            value = (g + 0.95 * moved).astype(jnp.bfloat16)
            steer[m, 0] = value[:, :half]
            steer[m, 1] = value[:, half:]


def steer_pieces(momentum, gradient):
    mats, rows, width = momentum.shape
    shape = (mats, 2, rows, width // 2)
    anywhere = pl.BlockSpec(memory_space=pl.ANY)
    inside = pl.BlockSpec(memory_space=pltpu.VMEM)
    dma = pltpu.SemaphoreType.DMA((STEER_PARTS,))
    quarter = jax.ShapeDtypeStruct((mats // AFTER_PARTS, rows, width), jnp.float32)
    *afters, steer = pl.pallas_call(
        steer_kernel,
        out_shape=(
            *[quarter] * AFTER_PARTS,
            jax.ShapeDtypeStruct(shape, jnp.bfloat16),
        ),
        in_specs=[anywhere] * 2,
        out_specs=(inside,) * (AFTER_PARTS + 1),
        scratch_shapes=[pltpu.VMEM(gradient.shape, jnp.bfloat16), dma, dma],
        compiler_params=pltpu.CompilerParams(vmem_limit_bytes=40 * MIB),
        cost_estimate=cost(4 * momentum.size, 8 * momentum.size),
        name="steer",
    )(momentum, gradient)
    return afters, steer.reshape(mats * 2, rows, width // 2)


def gram_kernel(group, x, own):
    start = 0
    for j in group:
        value = lax.dot_general(
            x[0 : (j + 1) * TILE],
            x[span(j)],
            (((1,), (1,)), ((), ())),
            preferred_element_type=jnp.float32,
        )
        at = slice(start, start + (j + 1) * TILE)
        start += (j + 1) * TILE
        own[at] = value


def gram_half(x, group, pairs):
    rows, part = x.shape
    shape = (len(pairs) * TILE, TILE)
    return pl.pallas_call(
        functools.partial(gram_kernel, group),
        out_shape=jax.ShapeDtypeStruct(shape, jnp.float32),
        in_specs=[pl.BlockSpec(memory_space=pltpu.VMEM)],
        compiler_params=pltpu.CompilerParams(vmem_limit_bytes=16 * MIB),
        cost_estimate=cost(2 * len(pairs) * TILE * TILE * part, rows * part * 2 + len(pairs) * TILE * TILE * 6),
        name="gram",
    )(x)


def update_kernel(x, *rest):
    owns, others, rest = rest[: len(GROUPS)], rest[len(GROUPS) : 2 * len(GROUPS)], rest[2 * len(GROUPS) :]
    afters = rest[:AFTER_PARTS]
    out, stored, g, h, s, w, m0, m1, wide0, wide1, after_sem = rest[AFTER_PARTS:]
    storing = []
    for c, after in enumerate(afters):
        share = after.shape[0]
        copy = pltpu.make_async_copy(after, stored.at[pl.ds(c * share, share)], after_sem.at[c])
        copy.start()
        storing.append(copy)
    here = lax.broadcasted_iota(jnp.int32, (TILE, TILE), 0) == lax.broadcasted_iota(
        jnp.int32, (TILE, TILE), 1
    )
    total = jnp.zeros((1, 1), jnp.float32)
    for own, other, pairs in zip(owns, others, PAIRS):
        for k, (i, j) in enumerate(pairs):
            block = own[span(k)] + other[span(k)]
            wide0[span(i), span(j)] = block
            narrow = block.astype(jnp.bfloat16)
            g[span(i), span(j)] = narrow
            if i == j:
                block = jnp.where(here, block, 0.0)
                block = jnp.sum(block, axis=0, keepdims=True)
                total = total + jnp.sum(block, axis=1, keepdims=True)
            else:
                g[span(j), span(i)] = narrow.T
    inverse = 1.0 / (jnp.sqrt(total) + 1e-07)
    factor = inverse * FACTOR
    direct = LINEAR**3 * factor
    square = inverse * inverse

    def product(left, right, store, rest, keep=None):
        lost = [None] * SIDE
        for j in reversed(range(SIDE)):
            at = (slice(0, (j + 1) * TILE), span(j))
            value = jnp.dot(left[at[0], :], right[:, at[1]], preferred_element_type=jnp.float32)
            value = rest(value, at, j)
            if keep is not None:
                keep[at] = value
            narrow = value.astype(jnp.bfloat16)
            store[at] = narrow
            for i in range(j):
                store[span(j), span(i)] = narrow[span(i)].T
            lost[j] = jnp.where(here, value[span(j)] - narrow[span(j)].astype(jnp.float32), 0.0)
        return lost

    def wide(ref, at):
        return ref[at].astype(jnp.float32)


    product(g, g, m0, lambda v, at, j: square * (CUBIC * wide(g, at) + square * (QUINTIC * v)))
    product(m0, g, w, lambda v, at, j: square * (LINEAR * wide0[at] + v), wide1)
    product(m0, w, h, lambda v, at, j: LINEAR * wide1[at] + v, wide0)
    product(h, h, m1, lambda v, at, j: CUBIC * wide(h, at) + QUINTIC * v)
    product(m1, h, w, lambda v, at, j: LINEAR * wide0[at] + v, wide1)
    product(m1, w, g, lambda v, at, j: LINEAR * wide1[at] + v)
    lost = product(m1, m0, s, lambda v, at, j: LINEAR * (wide(m0, at) + wide(m1, at)) + v)
    across = [jnp.sum(block, axis=0, keepdims=True) for block in lost]
    down = [LINEAR * jnp.sum(block, axis=1, keepdims=True) for block in lost]
    product(g, g, m0, lambda v, at, j: CUBIC * wide(g, at) + QUINTIC * v)
    lost = product(
        m0,
        s,
        h,
        lambda v, at, j: factor
        * (LINEAR * wide(s, at) + (LINEAR * LINEAR + across[j]) * wide(m0, at) + v),
    )
    for i in reversed(range(SIDE)):
        value = jnp.dot(h[span(i), :], x[...], preferred_element_type=jnp.float32)
        diagonal = direct + factor * down[i] + jnp.sum(lost[i], axis=1, keepdims=True)
        out[span(i)] = (value + diagonal * x[span(i)].astype(jnp.float32)).astype(jnp.bfloat16)
    for copy in storing:
        copy.wait()


def update_half(x, owns, others, afters):
    n, part = x.shape
    anywhere = pl.BlockSpec(memory_space=pl.ANY)
    inside = pl.BlockSpec(memory_space=pltpu.VMEM)
    square = pltpu.VMEM((n, n), jnp.bfloat16)
    return pl.pallas_call(
        update_kernel,
        out_shape=(
            jax.ShapeDtypeStruct((n, part), jnp.bfloat16),
            jax.ShapeDtypeStruct((afters[0].shape[0] * AFTER_PARTS, *afters[0].shape[1:]), jnp.float32),
        ),
        in_specs=[inside, *[inside] * (2 * len(GROUPS)), *[anywhere] * AFTER_PARTS],
        out_specs=(inside, anywhere),
        scratch_shapes=[
            *[square] * 6,
            *[pltpu.VMEM((n, n), jnp.float32)] * 2,
            pltpu.SemaphoreType.DMA((AFTER_PARTS,)),
        ],
        compiler_params=pltpu.CompilerParams(vmem_limit_bytes=30 * MIB),
        cost_estimate=cost(2 * n * n * (9 * n + part), n * part * 4 + n * n * 6),
        name="update",
    )(x, *owns, *others, *afters)


def exchange(x):
    return lax.all_to_all(x, "fsdp", split_axis=0, concat_axis=0, tiled=True)


def local(momentum, gradient):
    count = lax.axis_size("fsdp")
    mats, rows, width = momentum.shape
    half = width // 2
    afters, pieces = steer_pieces(momentum, gradient)
    x = exchange(pieces).reshape(count * rows, half)
    owns, others = [], []
    for group, pairs in zip(GROUPS, PAIRS):
        own = gram_half(x, group, pairs)
        owns.append(own)
        others.append(partner(own, "fsdp", 0))
    outgoing, new_momentum = update_half(x, owns, others, afters)
    returned = exchange(outgoing.reshape(count, rows, half))
    update = returned.reshape(mats, 2, rows, half).transpose(0, 2, 1, 3).reshape(mats, rows, width)
    return (new_momentum, update)


def solution(mesh):
    return jax.shard_map(
        local,
        mesh=mesh,
        in_specs=(P(None, "fsdp", None), P(None, "fsdp", None)),
        out_specs=(P(None, "fsdp", None), P(None, "fsdp", None)),
        check_vma=False,
    )
```

```python
import functools

import jax
import jax.numpy as jnp
from jax import lax
from jax.experimental import pallas as pl
from jax.experimental.pallas import tpu as pltpu
from jax.sharding import PartitionSpec as P

D = 3584
FF = 1024
ITERS = 3
LINEAR, CUBIC, QUINTIC = 3.4445, -4.775, 2.0315
FACTOR = 0.2 * max(FF, D) ** 0.5
TILE = 256
SIDE = FF // TILE
HALF = TILE // 2
GROUPS = [(2, 1, 0), (3,)]
PAIRS = [[(i, j) for j in group for i in range(j + 1)] for group in GROUPS]
MIB = 2**20


def cost(flops, moved):
    return pl.CostEstimate(flops=flops, bytes_accessed=moved, transcendentals=0)


def span(i, size=TILE):
    return slice(i * size, (i + 1) * size)


def partner(x, axis, apart):
    return lax.ppermute(x, axis, [(i, i ^ 1 << apart) for i in range(lax.axis_size(axis))])


STEER_PARTS = 8
AFTER_PARTS = 4


def steer_kernel(momentum, gradient, *rest):
    afters, (steer, g_buf, m_sem, g_sem) = rest[:AFTER_PARTS], rest[AFTER_PARTS:]
    mats, rows, width = g_buf.shape
    half = width // 2
    group = mats // STEER_PARTS
    share = STEER_PARTS // AFTER_PARTS
    arriving = []
    for c in range(STEER_PARTS):
        at = pl.ds(c * group, group)
        after = afters[c // share].at[pl.ds(c % share * group, group)]
        pair = (
            pltpu.make_async_copy(momentum.at[at], after, m_sem.at[c]),
            pltpu.make_async_copy(gradient.at[at], g_buf.at[at], g_sem.at[c]),
        )
        for copy in pair:
            copy.start()
        arriving.append(pair)
    for c in range(STEER_PARTS):
        for copy in arriving[c]:
            copy.wait()

        after = afters[c // share]

        @pl.loop(0, group)
        def _(i):
            m = c * group + i
            place = c % share * group + i
            g = g_buf[m].astype(jnp.float32)
            moved = 0.95 * after[place] + g
            after[place] = moved
            value = (g + 0.95 * moved).astype(jnp.bfloat16)
            steer[m, 0] = value[:, :half]
            steer[m, 1] = value[:, half:]


def steer_pieces(momentum, gradient):
    mats, rows, width = momentum.shape
    shape = (mats, 2, rows, width // 2)
    anywhere = pl.BlockSpec(memory_space=pl.ANY)
    inside = pl.BlockSpec(memory_space=pltpu.VMEM)
    dma = pltpu.SemaphoreType.DMA((STEER_PARTS,))
    quarter = jax.ShapeDtypeStruct((mats // AFTER_PARTS, rows, width), jnp.float32)
    *afters, steer = pl.pallas_call(
        steer_kernel,
        out_shape=(
            *[quarter] * AFTER_PARTS,
            jax.ShapeDtypeStruct(shape, jnp.bfloat16),
        ),
        in_specs=[anywhere] * 2,
        out_specs=(inside,) * (AFTER_PARTS + 1),
        scratch_shapes=[pltpu.VMEM(gradient.shape, jnp.bfloat16), dma, dma],
        compiler_params=pltpu.CompilerParams(vmem_limit_bytes=40 * MIB),
        cost_estimate=cost(4 * momentum.size, 8 * momentum.size),
        name="steer",
    )(momentum, gradient)
    return afters, steer.reshape(mats * 2, rows, width // 2)


def starts(group):
    found = [0]
    for j in group:
        for i in range(j + 1):
            found.append(found[-1] + (HALF if i == j else TILE) + TILE)
    return found


def gram_kernel(group, x, own):
    places = dict(zip(((i, j) for j in group for i in range(j + 1)), starts(group)))
    for j in group:
        value = lax.dot_general(
            x[0 : (j + 1) * TILE],
            x[span(j)],
            (((1,), (1,)), ((), ())),
            preferred_element_type=jnp.float32,
        )
        for i in range(j + 1):
            block, first = value[span(i)], places[i, j]
            left = HALF if i == j else TILE
            own[first : first + left] = block[:left, :HALF]
            own[first + left : first + left + TILE] = block[:, HALF:]


def gram_half(x, group, pairs):
    rows, part = x.shape
    shape = (starts(group)[-1], HALF)
    return pl.pallas_call(
        functools.partial(gram_kernel, group),
        out_shape=jax.ShapeDtypeStruct(shape, jnp.float32),
        in_specs=[pl.BlockSpec(memory_space=pltpu.VMEM)],
        compiler_params=pltpu.CompilerParams(vmem_limit_bytes=16 * MIB),
        cost_estimate=cost(2 * len(pairs) * TILE * TILE * part, rows * part * 2 + len(pairs) * TILE * TILE * 6),
        name="gram",
    )(x)


def update_kernel(x, *rest):
    owns, others, rest = rest[: len(GROUPS)], rest[len(GROUPS) : 2 * len(GROUPS)], rest[2 * len(GROUPS) :]
    afters = rest[:AFTER_PARTS]
    out, stored, g, h, s, w, m0, m1, wide0, wide1, after_sem = rest[AFTER_PARTS:]
    storing = []
    for c, after in enumerate(afters):
        share = after.shape[0]
        copy = pltpu.make_async_copy(after, stored.at[pl.ds(c * share, share)], after_sem.at[c])
        copy.start()
        storing.append(copy)
    here = lax.broadcasted_iota(jnp.int32, (TILE, TILE), 0) == lax.broadcasted_iota(
        jnp.int32, (TILE, TILE), 1
    )
    total = jnp.zeros((1, 1), jnp.float32)
    for own, other, pairs, group in zip(owns, others, PAIRS, GROUPS):
        for (i, j), first in zip(pairs, starts(group)):
            left = HALF if i == j else TILE
            row, column = i * TILE, j * TILE
            near = own[first : first + left] + other[first : first + left]
            at = slice(first + left, first + left + TILE)
            far = own[at] + other[at]
            corners = ((row, column, near), (row, column + HALF, far))
            if i == j:
                for block in (near, far[HALF:]):
                    block = jnp.where(here[:HALF, :HALF], block, 0.0)
                    block = jnp.sum(block, axis=0, keepdims=True)
                    total = total + jnp.sum(block, axis=1, keepdims=True)
                corners = (*corners, (row + HALF, column, far[:HALF].T))
            for r, c, block in corners:
                at = (slice(r, r + block.shape[0]), slice(c, c + HALF))
                wide0[at] = block
                g[at] = block.astype(jnp.bfloat16)
                if i != j:
                    g[at[1], at[0]] = block.astype(jnp.bfloat16).T
    inverse = 1.0 / (jnp.sqrt(total) + 1e-07)
    factor = inverse * FACTOR
    direct = LINEAR**3 * factor
    square = inverse * inverse

    def product(left, right, store, rest, keep=None):
        lost = [None] * SIDE
        for j in reversed(range(SIDE)):
            at = (slice(0, (j + 1) * TILE), span(j))
            value = jnp.dot(left[at[0], :], right[:, at[1]], preferred_element_type=jnp.float32)
            value = rest(value, at, j)
            if keep is not None:
                keep[at] = value
            narrow = value.astype(jnp.bfloat16)
            store[at] = narrow
            for i in range(j):
                store[span(j), span(i)] = narrow[span(i)].T
            lost[j] = jnp.where(here, value[span(j)] - narrow[span(j)].astype(jnp.float32), 0.0)
        return lost

    def wide(ref, at):
        return ref[at].astype(jnp.float32)


    product(g, g, m0, lambda v, at, j: square * (CUBIC * wide(g, at) + square * (QUINTIC * v)))
    product(m0, g, w, lambda v, at, j: square * (LINEAR * wide0[at] + v), wide1)
    product(m0, w, h, lambda v, at, j: LINEAR * wide1[at] + v, wide0)
    product(h, h, m1, lambda v, at, j: CUBIC * wide(h, at) + QUINTIC * v)
    product(m1, h, w, lambda v, at, j: LINEAR * wide0[at] + v, wide1)
    product(m1, w, g, lambda v, at, j: LINEAR * wide1[at] + v)
    lost = product(m1, m0, s, lambda v, at, j: LINEAR * (wide(m0, at) + wide(m1, at)) + v)
    across = [jnp.sum(block, axis=0, keepdims=True) for block in lost]
    down = [LINEAR * jnp.sum(block, axis=1, keepdims=True) for block in lost]
    product(g, g, m0, lambda v, at, j: CUBIC * wide(g, at) + QUINTIC * v)
    lost = product(
        m0,
        s,
        h,
        lambda v, at, j: factor
        * (LINEAR * wide(s, at) + (LINEAR * LINEAR + across[j]) * wide(m0, at) + v),
    )
    for i in reversed(range(SIDE)):
        value = jnp.dot(h[span(i), :], x[...], preferred_element_type=jnp.float32)
        diagonal = direct + factor * down[i] + jnp.sum(lost[i], axis=1, keepdims=True)
        out[span(i)] = (value + diagonal * x[span(i)].astype(jnp.float32)).astype(jnp.bfloat16)
    for copy in storing:
        copy.wait()


def update_half(x, owns, others, afters):
    n, part = x.shape
    anywhere = pl.BlockSpec(memory_space=pl.ANY)
    inside = pl.BlockSpec(memory_space=pltpu.VMEM)
    square = pltpu.VMEM((n, n), jnp.bfloat16)
    return pl.pallas_call(
        update_kernel,
        out_shape=(
            jax.ShapeDtypeStruct((n, part), jnp.bfloat16),
            jax.ShapeDtypeStruct((afters[0].shape[0] * AFTER_PARTS, *afters[0].shape[1:]), jnp.float32),
        ),
        in_specs=[inside, *[inside] * (2 * len(GROUPS)), *[anywhere] * AFTER_PARTS],
        out_specs=(inside, anywhere),
        scratch_shapes=[
            *[square] * 6,
            *[pltpu.VMEM((n, n), jnp.float32)] * 2,
            pltpu.SemaphoreType.DMA((AFTER_PARTS,)),
        ],
        compiler_params=pltpu.CompilerParams(vmem_limit_bytes=30 * MIB),
        cost_estimate=cost(2 * n * n * (9 * n + part), n * part * 4 + n * n * 6),
        name="update",
    )(x, *owns, *others, *afters)


def exchange(x):
    return lax.all_to_all(x, "fsdp", split_axis=0, concat_axis=0, tiled=True)


def local(momentum, gradient):
    count = lax.axis_size("fsdp")
    mats, rows, width = momentum.shape
    half = width // 2
    afters, pieces = steer_pieces(momentum, gradient)
    x = exchange(pieces).reshape(count * rows, half)
    owns, others = [], []
    for group, pairs in zip(GROUPS, PAIRS):
        own = gram_half(x, group, pairs)
        owns.append(own)
        others.append(partner(own, "fsdp", 0))
    outgoing, new_momentum = update_half(x, owns, others, afters)
    returned = exchange(outgoing.reshape(count, rows, half))
    update = returned.reshape(mats, 2, rows, half).transpose(0, 2, 1, 3).reshape(mats, rows, width)
    return (new_momentum, update)


def solution(mesh):
    return jax.shard_map(
        local,
        mesh=mesh,
        in_specs=(P(None, "fsdp", None), P(None, "fsdp", None)),
        out_specs=(P(None, "fsdp", None), P(None, "fsdp", None)),
        check_vma=False,
    )
```
